32 devices in a mesh: tm: 8 (over z, x), space: 4 (over y, core).
Axes of the slice: x: 2, y: 2, z: 4, core: 2. Of those that a mesh axis runs over, the one named last changes fastest.
Arguments:
- queries: bfloat16 [8, 2560, 2240], P('tm', 'space'), may hold values from -6 to 6
- keys: bfloat16 [8, 2560, 2240], P('tm', 'space'), may hold values from -6 to 6
- values: bfloat16 [8, 2560, 2240], P('tm', 'space'), may hold values from -6 to 6
- gain: float32 [2240], replicated, may hold values from 0.1 to 1.9
- out_weight: bfloat16 [2240, 2240], P('tm'), may hold values from -0.125 to 0.125
Outputs:
- projected: bfloat16 [8, 2560, 2240], P('tm', 'space')
The draws below stay inside these ranges and needn't reach their ends.
All inputs are finite; a program needn't handle non-finite values.
Results may differ from the reference program's by a relative error of at most 0.0075.
Values may be sent and summed in bfloat16 or wider, within the bound.
A program may use at most 128 MiB of HBM per device.

```python
import jax
import jax.numpy as jnp
from jax import lax

HEADS = 20
HEAD_DIM = 112
D = 2240
BLOCKS = 8
SPATIAL = 2560


def levels(stream_key, extent, split, smallest, largest):
    level = 1.0
    for axis_at, blocks in split:
        draws = jax.random.uniform(jax.random.fold_in(jax.random.fold_in(stream_key, 6), axis_at), (blocks,), jnp.float32, smallest / len(split), largest / len(split))
        level = level * jnp.repeat(jnp.exp(draws), extent[axis_at] // blocks).reshape((-1,) + (1,) * (len(extent) - 1 - axis_at))
    return level


def scatter_about(own_key, dims, deviation, limit, shards=(), kind=jnp.bfloat16):
    loudness = levels(own_key, dims, shards, -0.22, 0.18) if shards else 1.0
    entries = jax.random.normal(own_key, dims, jnp.float32) * deviation * loudness
    return jnp.minimum(jnp.maximum(entries, -limit), limit).astype(kind)


def setup_inputs(seed: int = 0) -> dict:
    seeds = jax.random.split(jax.random.key(seed), 6)
    return {
        "queries": scatter_about(seeds[0], (BLOCKS, SPATIAL, D), 1.0, 6.0, ((0, 8), (1, 4))),
        "keys": scatter_about(seeds[1], (BLOCKS, SPATIAL, D), 1.0, 6.0, ((0, 8), (1, 4))),
        "values": scatter_about(seeds[2], (BLOCKS, SPATIAL, D), 1.0, 6.0, ((0, 8), (1, 4))),
        "gain": jnp.clip(1.0 + 0.18 * jax.random.normal(seeds[3], (D,), jnp.float32), 0.1, 1.9),
        "out_weight": scatter_about(seeds[4], (D, D), D ** -0.5, 0.125, ((0, 8),)),
    }


def reference(queries, keys, values, gain, out_weight):

    def block_stats(pair):
        fk = jnp.maximum(pair[0], 0).astype(jnp.float32).reshape(SPATIAL, HEADS, HEAD_DIM)
        vals = pair[1].astype(jnp.float32).reshape(SPATIAL, HEADS, HEAD_DIM)
        state = jnp.einsum('shi,shj->hij', fk, vals, precision=lax.Precision.HIGHEST)
        return (state, lax.optimization_barrier(jnp.sum(fk, axis=0)))
    states, norms = lax.map(block_stats, (keys, values))
    states = jnp.cumsum(states, axis=0)
    norms = jnp.cumsum(norms, axis=0)

    def read_block(triple):
        fq = jnp.maximum(triple[0], 0).astype(jnp.float32).reshape(SPATIAL, HEADS, HEAD_DIM)
        numer = jnp.einsum('shi,hij->shj', fq, triple[1], precision=lax.Precision.HIGHEST)
        denom = jnp.einsum('shi,hi->sh', fq, triple[2], precision=lax.Precision.HIGHEST) + 1.0
        mixed = (numer / denom[:, :, None]).reshape(SPATIAL, D)
        meansq = lax.optimization_barrier(jnp.mean(mixed * mixed, axis=-1, keepdims=True))
        normed = (mixed * lax.rsqrt(meansq + 1e-06) * gain).astype(jnp.bfloat16)
        return jnp.dot(normed, out_weight, preferred_element_type=jnp.float32).astype(jnp.bfloat16)
    return lax.map(read_block, (queries, states, norms))
```

```python
import functools

import jax
import jax.numpy as jnp
from jax import lax
from jax.experimental import pallas as pl
from jax.experimental.pallas import tpu as pltpu
from jax.sharding import PartitionSpec as P

HEADS = 20
LANES = 128
MESH = pl.DeviceIdType.MESH


def heads_of(tile, width, dim):
    first = tile * LANES
    last = min(first + LANES, width) - 1
    return range(first // dim, last // dim + 1)


def window(tile, width):
    return max(0, (tile - 1) * LANES), min(width, (tile + 2) * LANES)


def head_lanes(tile, dim):
    column = tile * LANES + lax.broadcasted_iota(jnp.int32, (dim, LANES), 1)
    return column // dim


def state_kernel(dim, k_ref, v_ref, out_ref):
    rows, width = k_ref.shape
    tiles = -(-width // LANES)
    spare = width - (tiles - 1) * LANES
    lane = lax.broadcasted_iota(jnp.int32, (dim, LANES), 1)
    ones = jnp.ones((rows, LANES), jnp.bfloat16)
    norms = jnp.zeros((dim, LANES), jnp.float32)
    done = set()
    for t in range(tiles):
        lo, hi = window(t, width)
        fk = jnp.maximum(k_ref[:, lo:hi], 0)
        end = min((t + 1) * LANES, width)
        v = v_ref[:, t * LANES : end]
        if end - t * LANES < LANES:
            v = jnp.concatenate(
                [v, jnp.zeros((rows, (t + 1) * LANES - end), v.dtype)], axis=1
            )
        both = lax.dot_general(
            fk,
            jnp.concatenate([v, ones], axis=1),
            (((0,), (0,)), ((), ())),
            preferred_element_type=jnp.float32,
        )
        owner = head_lanes(t, dim)
        compact = jnp.zeros((dim, LANES), jnp.float32)
        for h in heads_of(t, width, dim):
            at = h * dim - lo
            compact = jnp.where(owner == h, both[at : at + dim, :LANES], compact)
            if h not in done:
                done.add(h)
                norms = jnp.where(lane == spare + h, both[at : at + dim, LANES:], norms)
        if t == tiles - 1:
            compact = jnp.where(lane >= spare, norms, compact)
        out_ref[t] = compact.astype(out_ref.dtype)
    for t in range(tiles, out_ref.shape[0]):
        out_ref[t] = jnp.zeros((dim, LANES), out_ref.dtype)


def exchange_kernel(
    n, space, part_ref, w_ref, state_ref, wg_ref,
    landed, totals, arrived,
    local_sem, rs_send, rs_recv, scan_send, scan_recv, ag_send, ag_recv,
    tm_send, tm_recv, y_send, y_recv, core_send, core_recv,
):
    t = lax.axis_index("tm")
    s = lax.axis_index("space")
    cores = 2
    ys = space // cores
    y, c = s // cores, s % cores
    bits = []
    d = 1
    while d < n:
        bits.append(d)
        d *= 2

    def flip(m):
        where = t
        for d in bits:
            if m & d:
                where = where + d - 2 * d * ((t // d) % 2)
        return where

    def peer(r):
        return (t, lax.rem(s + r, space))

    barrier = pltpu.get_barrier_semaphore()
    for r in range(1, space):
        pl.semaphore_signal(barrier, inc=1, device_id=peer(r), device_id_type=MESH)
    for d in bits:
        pl.semaphore_signal(barrier, inc=1, device_id=(flip(d), s), device_id_type=MESH)
    pl.semaphore_wait(barrier, space - 1 + len(bits))

    sent = []

    def remote(src, dst, send, recv, device):
        return pltpu.make_async_remote_copy(
            src_ref=src, dst_ref=dst, send_sem=send, recv_sem=recv,
            device_id=device, device_id_type=MESH,
        )

    def go(copy):
        copy.start()
        sent.append(copy)

    for r in range(1, space):
        go(remote(part_ref.at[lax.rem(s + r, space)], landed.at[r],
                  rs_send.at[r], rs_recv.at[r], peer(r)))

    groups = (s, space + c)

    def weight_hop(i, m, d):
        g = groups[i]
        src = w_ref.at[g] if m == 0 else wg_ref.at[g, flip(m)]
        return remote(src, wg_ref.at[g, flip(m)], tm_send.at[i, m + d],
                      tm_recv.at[i, m + d], (flip(d), s))

    def await_weight(i, m):
        low = m & -m
        shard = wg_ref.at[groups[i], flip(m)]
        remote(shard, shard, tm_send.at[i, m], tm_recv.at[i, m], (flip(low), s)).wait_recv()

    def to_core(i, g, m):
        shard = wg_ref.at[g, flip(m)]
        return remote(shard, shard, core_send.at[i, m], core_recv.at[i, m],
                      (t, y * cores + (1 - c)))

    def to_y(r, m):
        shard = wg_ref.at[s, flip(m)]
        return remote(shard, shard, y_send.at[r, m], y_recv.at[r, m],
                      (t, lax.rem(y + r, ys) * cores + c))

    def from_y(r):
        return lax.rem(y + ys - r, ys) * cores + c

    for d in reversed(bits):
        for i in range(2):
            go(weight_hop(i, 0, d))
    own = pltpu.make_async_copy(w_ref, wg_ref.at[:, t], local_sem)
    own.start()

    pending = []

    def pass_on(m):
        for i in range(2):
            await_weight(i, m)
            for d in reversed(bits):
                if d < (m & -m):
                    go(weight_hop(i, m, d))
            if i == 0:
                for r in range(1, ys):
                    go(to_y(r, m))
            go(to_core(i, groups[i], m))
        pending.append(m)

    def settle(m):
        for r in range(1, ys):
            shard = wg_ref.at[from_y(r), flip(m)]
            remote(shard, shard, y_send.at[r, m], y_recv.at[r, m],
                   (t, lax.rem(y + ys - r, ys) * cores + c)).wait_recv()
            go(to_core(1 + r, from_y(r), m))

    order = sorted(range(1, n), key=lambda m: (bin(m).count("1"), -m))
    order = list(order)

    def next_weight():
        if order:
            pass_on(order.pop(0))

    total = part_ref[s].astype(jnp.float32)
    for r in range(1, space):
        remote(part_ref.at[0], landed.at[r], rs_send.at[r], rs_recv.at[r], peer(r)).wait_recv()
        total = total + landed[r].astype(jnp.float32)
    prefix = total
    for k, d in enumerate(bits):
        totals[k] = total.astype(totals.dtype)
        hop = remote(totals.at[k], arrived.at[k], scan_send.at[k], scan_recv.at[k], (flip(d), s))
        go(hop)
        next_weight()
        hop.wait_recv()
        got = arrived[k].astype(jnp.float32)
        prefix = prefix + got * ((t // d) % 2).astype(jnp.float32)
        total = total + got
    state_ref[s] = prefix.astype(state_ref.dtype)
    for r in range(1, space):
        go(remote(state_ref.at[s], state_ref.at[s], ag_send.at[r], ag_recv.at[r], peer(r)))
    while order:
        next_weight()
        if len(pending) > 1:
            settle(pending.pop(0))
    while pending:
        settle(pending.pop(0))
    for r in range(1, space):
        slot = state_ref.at[lax.rem(s + space - r, space)]
        remote(slot, slot, ag_send.at[r], ag_recv.at[r], peer(r)).wait_recv()
    other = 1 - c
    for m in range(1, n):
        sources = [y * cores + other, space + other]
        sources += [lax.rem(y + ys - r, ys) * cores + other for r in range(1, ys)]
        for i, g in enumerate(sources):
            shard = wg_ref.at[g, flip(m)]
            remote(shard, shard, core_send.at[i, m], core_recv.at[i, m],
                   (t, y * cores + other)).wait_recv()
    own.wait()
    for copy in sent:
        copy.wait_send()


def read_kernel(dim, q_ref, state_ref, gain_ref, w_ref, out_ref, mixed, normed):
    rows, width = q_ref.shape
    tiles = -(-width // LANES)
    spare = width - (tiles - 1) * LANES

    @pl.when(pl.program_id(0) == 0)
    def _():
        lane = lax.broadcasted_iota(jnp.int32, (dim, LANES), 1)
        norms = state_ref[tiles - 1].astype(jnp.float32)
        squares = jnp.zeros((rows, LANES), jnp.float32)
        for t in range(tiles):
            lo, hi = window(t, width)
            owner = head_lanes(t, dim)
            part = state_ref[t].astype(jnp.float32)
            rows_of = []
            at = lo
            for h in heads_of(t, width, dim):
                if h * dim > at:
                    rows_of.append(jnp.zeros((h * dim - at, 2 * LANES), jnp.bfloat16))
                norm = jnp.sum(jnp.where(lane == spare + h, norms, 0), axis=1, keepdims=True)
                mine = owner == h
                rows_of.append(
                    jnp.concatenate(
                        [jnp.where(mine, part, 0), jnp.where(mine, norm, 0)], axis=1
                    ).astype(jnp.bfloat16)
                )
                at = (h + 1) * dim
            if at < hi:
                rows_of.append(jnp.zeros((hi - at, 2 * LANES), jnp.bfloat16))
            fq = jnp.maximum(q_ref[:, lo:hi], 0)
            both = jnp.dot(
                fq, jnp.concatenate(rows_of, axis=0), preferred_element_type=jnp.float32
            )
            tile = both[:, :LANES] / (both[:, LANES:] + 1.0)
            mixed[:, t * LANES : (t + 1) * LANES] = tile
            squares = squares + tile * tile
        meansq = jnp.sum(squares, axis=1, keepdims=True) / width
        scale = lax.rsqrt(meansq + 1e-06)
        for t in range(tiles):
            end = min((t + 1) * LANES, width)
            normed[:, t * LANES : end] = (
                mixed[:, t * LANES : end] * scale * gain_ref[:, t * LANES : end]
            ).astype(normed.dtype)

    out_ref[...] = jnp.dot(
        normed[...], w_ref[0], preferred_element_type=jnp.float32
    ).astype(out_ref.dtype)


def local(n, space, queries, keys, values, gain, out_weight):
    _, rows, width = queries.shape
    dim = width // HEADS
    tiles = -(-width // LANES)
    share = -(-tiles // space)
    shard, columns = out_weight.shape
    groups = space + 2
    gw = -(-columns // (groups * LANES)) * LANES
    vmem = pl.BlockSpec(memory_space=pltpu.VMEM)
    big = pltpu.CompilerParams(vmem_limit_bytes=56 * 1024 * 1024)

    w = jnp.pad(out_weight, ((0, 0), (0, groups * gw - columns)))
    w = w.reshape(shard, groups, gw).transpose(1, 0, 2)

    state = pl.pallas_call(
        functools.partial(state_kernel, dim),
        out_shape=jax.ShapeDtypeStruct((space * share, dim, LANES), jnp.bfloat16),
        in_specs=[vmem, vmem],
        out_specs=vmem,
        compiler_params=big,
        name="block_state",
    )(keys[0], values[0])

    steps = n.bit_length() - 1
    dma = pltpu.SemaphoreType.DMA
    piece = (share, dim, LANES)
    prefix, wg = pl.pallas_call(
        functools.partial(exchange_kernel, n, space),
        out_shape=(
            jax.ShapeDtypeStruct((space,) + piece, jnp.bfloat16),
            jax.ShapeDtypeStruct((groups, n, shard, gw), jnp.bfloat16),
        ),
        in_specs=[vmem, pl.BlockSpec(memory_space=pl.ANY)],
        out_specs=(vmem, pl.BlockSpec(memory_space=pl.ANY)),
        scratch_shapes=[
            pltpu.VMEM((space,) + piece, jnp.bfloat16),
            pltpu.VMEM((steps,) + piece, jnp.bfloat16),
            pltpu.VMEM((steps,) + piece, jnp.bfloat16),
            dma,
            dma((space,)), dma((space,)),
            dma((steps,)), dma((steps,)),
            dma((space,)), dma((space,)),
            dma((2, n)), dma((2, n)),
            dma((space // 2, n)), dma((space // 2, n)),
            dma((space // 2 + 1, n)), dma((space // 2 + 1, n)),
        ],
        compiler_params=pltpu.CompilerParams(
            collective_id=0, has_side_effects=True, vmem_limit_bytes=56 * 1024 * 1024
        ),
        name="exchange",
    )(state.reshape((space,) + piece), w)

    out = pl.pallas_call(
        functools.partial(read_kernel, dim),
        grid=(-(-columns // gw),),
        out_shape=jax.ShapeDtypeStruct((rows, columns), jnp.bfloat16),
        in_specs=[
            pl.BlockSpec((rows, width), lambda i: (0, 0)),
            pl.BlockSpec((space * share, dim, LANES), lambda i: (0, 0, 0)),
            pl.BlockSpec((1, width), lambda i: (0, 0)),
            pl.BlockSpec((1, n * shard, gw), lambda i: (i, 0, 0)),
        ],
        out_specs=pl.BlockSpec((rows, gw), lambda i: (0, i)),
        scratch_shapes=[
            pltpu.VMEM((rows, tiles * LANES), jnp.float32),
            pltpu.VMEM((rows, width), jnp.bfloat16),
        ],
        compiler_params=big,
        name="read_project",
    )(
        queries[0],
        prefix.reshape(space * share, dim, LANES),
        gain.reshape(1, width),
        wg.reshape(groups, n * shard, gw),
    )
    return out[None]


def solution(mesh):
    sizes = dict(mesh.shape)
    return jax.shard_map(
        functools.partial(local, sizes["tm"], sizes["space"]),
        mesh=mesh,
        in_specs=(
            P("tm", "space", None),
            P("tm", "space", None),
            P("tm", "space", None),
            P(),
            P("tm", None),
        ),
        out_specs=P("tm", "space", None),
        check_vma=False,
    )
```

```python
import functools

import jax
import jax.numpy as jnp
from jax import lax
from jax.experimental import pallas as pl
from jax.experimental.pallas import tpu as pltpu
from jax.sharding import PartitionSpec as P

HEADS = 20
LANES = 128
MESH = pl.DeviceIdType.MESH


def exchange_kernel(
    n, space, k_ref, v_ref, w_ref, state_ref, wg_ref,
    keys, vals, ones, part_ref, landed, totals, arrived,
    local_sem, load_sem, rs_send, rs_recv, scan_send, scan_recv, ag_send, ag_recv,
    tm_send, tm_recv, y_send, y_recv, core_send, core_recv,
):
    t = lax.axis_index("tm")
    s = lax.axis_index("space")
    cores = 2
    ys = space // cores
    y, c = s // cores, s % cores
    bits = []
    d = 1
    while d < n:
        bits.append(d)
        d *= 2

    def flip(m):
        where = t
        for d in bits:
            if m & d:
                where = where + d - 2 * d * ((t // d) % 2)
        return where

    def peer(r):
        return (t, lax.rem(s + r, space))

    loads = [
        pltpu.make_async_copy(k_ref, keys, load_sem.at[0]),
        pltpu.make_async_copy(v_ref, vals, load_sem.at[1]),
    ]
    for load in loads:
        load.start()

    barrier = pltpu.get_barrier_semaphore()
    for r in range(1, space):
        pl.semaphore_signal(barrier, inc=1, device_id=peer(r), device_id_type=MESH)
    for d in bits:
        pl.semaphore_signal(barrier, inc=1, device_id=(flip(d), s), device_id_type=MESH)
    pl.semaphore_wait(barrier, space - 1 + len(bits))

    sent = []

    def remote(src, dst, send, recv, device):
        return pltpu.make_async_remote_copy(
            src_ref=src, dst_ref=dst, send_sem=send, recv_sem=recv,
            device_id=device, device_id_type=MESH,
        )

    def go(copy):
        copy.start()
        sent.append(copy)

    groups = (s, space + c)

    def weight_hop(i, m, d):
        g = groups[i]
        src = w_ref.at[g] if m == 0 else wg_ref.at[g, flip(m)]
        return remote(src, wg_ref.at[g, flip(m)], tm_send.at[i, m + d],
                      tm_recv.at[i, m + d], (flip(d), s))

    def await_weight(i, m):
        low = m & -m
        shard = wg_ref.at[groups[i], flip(m)]
        remote(shard, shard, tm_send.at[i, m], tm_recv.at[i, m], (flip(low), s)).wait_recv()

    def to_core(i, g, m):
        shard = wg_ref.at[g, flip(m)]
        return remote(shard, shard, core_send.at[i, m], core_recv.at[i, m],
                      (t, y * cores + (1 - c)))

    def to_y(r, m):
        shard = wg_ref.at[s, flip(m)]
        return remote(shard, shard, y_send.at[r, m], y_recv.at[r, m],
                      (t, lax.rem(y + r, ys) * cores + c))

    def from_y(r):
        return lax.rem(y + ys - r, ys) * cores + c

    for d in reversed(bits):
        for i in range(2):
            go(weight_hop(i, 0, d))
    own = pltpu.make_async_copy(w_ref, wg_ref.at[:, t], local_sem)
    own.start()

    heads, dim, _ = keys.shape
    ones[...] = jnp.ones_like(ones)
    for load in loads:
        load.wait()
    share = part_ref.shape[1]

    def one_state(h):
        v = jnp.concatenate([vals[h], ones[...]], axis=0)
        fk = jnp.maximum(keys[h], 0)
        return lax.dot_general(
            v, fk, (((1,), (1,)), ((), ())), preferred_element_type=jnp.float32
        ).astype(part_ref.dtype)

    for h in range(space * share):
        part_ref[h // share, h % share] = (
            one_state(h) if h < heads else jnp.zeros(part_ref.shape[2:], part_ref.dtype)
        )

    for r in range(1, space):
        go(remote(part_ref.at[lax.rem(s + r, space)], landed.at[r],
                  rs_send.at[r], rs_recv.at[r], peer(r)))

    pending = []

    def pass_on(m):
        for i in range(2):
            await_weight(i, m)
            for d in reversed(bits):
                if d < (m & -m):
                    go(weight_hop(i, m, d))
            if i == 0:
                for r in range(1, ys):
                    go(to_y(r, m))
            go(to_core(i, groups[i], m))
        pending.append(m)

    def settle(m):
        for r in range(1, ys):
            shard = wg_ref.at[from_y(r), flip(m)]
            remote(shard, shard, y_send.at[r, m], y_recv.at[r, m],
                   (t, lax.rem(y + ys - r, ys) * cores + c)).wait_recv()
            go(to_core(1 + r, from_y(r), m))

    order = sorted(range(1, n), key=lambda m: (bin(m).count("1"), -m))
    order = list(order)

    def next_weight():
        if order:
            pass_on(order.pop(0))

    total = part_ref[s].astype(jnp.float32)
    for r in range(1, space):
        remote(part_ref.at[0], landed.at[r], rs_send.at[r], rs_recv.at[r], peer(r)).wait_recv()
        total = total + landed[r].astype(jnp.float32)
    prefix = total
    for k, d in enumerate(bits):
        totals[k] = total.astype(totals.dtype)
        hop = remote(totals.at[k], arrived.at[k], scan_send.at[k], scan_recv.at[k], (flip(d), s))
        go(hop)
        next_weight()
        hop.wait_recv()
        got = arrived[k].astype(jnp.float32)
        prefix = prefix + got * ((t // d) % 2).astype(jnp.float32)
        total = total + got
    state_ref[s] = prefix.astype(state_ref.dtype)
    for r in range(1, space):
        go(remote(state_ref.at[s], state_ref.at[s], ag_send.at[r], ag_recv.at[r], peer(r)))
    while order:
        next_weight()
        if len(pending) > 1:
            settle(pending.pop(0))
    while pending:
        settle(pending.pop(0))
    for r in range(1, space):
        slot = state_ref.at[lax.rem(s + space - r, space)]
        remote(slot, slot, ag_send.at[r], ag_recv.at[r], peer(r)).wait_recv()
    other = 1 - c
    for m in range(1, n):
        sources = [y * cores + other, space + other]
        sources += [lax.rem(y + ys - r, ys) * cores + other for r in range(1, ys)]
        for i, g in enumerate(sources):
            shard = wg_ref.at[g, flip(m)]
            remote(shard, shard, core_send.at[i, m], core_recv.at[i, m],
                   (t, y * cores + other)).wait_recv()
    own.wait()
    for copy in sent:
        copy.wait_send()


def read_kernel(q_ref, state_ref, gain_ref, w_ref, out_ref, mixed, normed):
    heads, dim, rows = q_ref.shape

    @pl.when(pl.program_id(0) == 0)
    def _():
        squares = jnp.zeros((1, rows), jnp.float32)
        for h in range(heads):
            both = jnp.dot(
                state_ref[h], jnp.maximum(q_ref[h], 0), preferred_element_type=jnp.float32
            )
            tile = both[:dim] / (both[dim : dim + 1] + 1.0)
            mixed[h] = tile
            squares = squares + jnp.sum(tile * tile, axis=0, keepdims=True)
        scale = lax.rsqrt(squares / (heads * dim) + 1e-06)
        for h in range(heads):
            mixed[h] = mixed[h] * scale * gain_ref[h]
        flat = mixed[...].reshape(heads * dim, rows).astype(normed.dtype)
        normed[...] = flat.T

    out_ref[...] = (
        jnp.dot(normed[...], w_ref[0], preferred_element_type=jnp.float32)
        .astype(out_ref.dtype)
        .T
    )


def local(n, space, queries, keys, values, gain, out_weight):
    _, rows, width = queries.shape
    dim = width // HEADS
    extra = 16
    share = -(-HEADS // space)
    shard, columns = out_weight.shape
    groups = space + 2
    gw = -(-columns // (groups * LANES)) * LANES
    vmem = pl.BlockSpec(memory_space=pltpu.VMEM)
    big = pltpu.CompilerParams(vmem_limit_bytes=56 * 1024 * 1024)

    w = jnp.pad(out_weight, ((0, 0), (0, groups * gw - columns)))
    w = w.reshape(shard, groups, gw).transpose(1, 0, 2)

    def by_head(a):
        return a[0].T.reshape(HEADS, dim, rows)

    steps = n.bit_length() - 1
    dma = pltpu.SemaphoreType.DMA
    piece = (share, dim + extra, dim)
    prefix, wg = pl.pallas_call(
        functools.partial(exchange_kernel, n, space),
        out_shape=(
            jax.ShapeDtypeStruct((space,) + piece, jnp.bfloat16),
            jax.ShapeDtypeStruct((groups, n, shard, gw), jnp.bfloat16),
        ),
        in_specs=[pl.BlockSpec(memory_space=pl.ANY)] * 3,
        out_specs=(vmem, pl.BlockSpec(memory_space=pl.ANY)),
        scratch_shapes=[
            pltpu.VMEM((HEADS, dim, rows), jnp.bfloat16),
            pltpu.VMEM((HEADS, dim, rows), jnp.bfloat16),
            pltpu.VMEM((extra, rows), jnp.bfloat16),
            pltpu.VMEM((space,) + piece, jnp.bfloat16),
            pltpu.VMEM((space,) + piece, jnp.bfloat16),
            pltpu.VMEM((steps,) + piece, jnp.bfloat16),
            pltpu.VMEM((steps,) + piece, jnp.bfloat16),
            dma,
            dma((2,)),
            dma((space,)), dma((space,)),
            dma((steps,)), dma((steps,)),
            dma((space,)), dma((space,)),
            dma((2, n)), dma((2, n)),
            dma((space // 2, n)), dma((space // 2, n)),
            dma((space // 2 + 1, n)), dma((space // 2 + 1, n)),
        ],
        compiler_params=pltpu.CompilerParams(
            collective_id=0, has_side_effects=True, vmem_limit_bytes=56 * 1024 * 1024
        ),
        name="exchange",
    )(by_head(keys), by_head(values), w)

    out = pl.pallas_call(
        read_kernel,
        grid=(-(-columns // gw),),
        out_shape=jax.ShapeDtypeStruct((columns, rows), jnp.bfloat16),
        in_specs=[
            pl.BlockSpec((HEADS, dim, rows), lambda i: (0, 0, 0)),
            pl.BlockSpec((space * share, dim + extra, dim), lambda i: (0, 0, 0)),
            pl.BlockSpec((HEADS, dim, 1), lambda i: (0, 0, 0)),
            pl.BlockSpec((1, n * shard, gw), lambda i: (i, 0, 0)),
        ],
        out_specs=pl.BlockSpec((gw, rows), lambda i: (i, 0)),
        scratch_shapes=[
            pltpu.VMEM((HEADS, dim, rows), jnp.float32),
            pltpu.VMEM((rows, width), jnp.bfloat16),
        ],
        compiler_params=big,
        name="read_project",
    )(
        by_head(queries),
        prefix.reshape((space * share,) + piece[1:]),
        gain.reshape(HEADS, dim, 1),
        wg.reshape(groups, n * shard, gw),
    )
    return out.T[None]


def solution(mesh):
    sizes = dict(mesh.shape)
    return jax.shard_map(
        functools.partial(local, sizes["tm"], sizes["space"]),
        mesh=mesh,
        in_specs=(
            P("tm", "space", None),
            P("tm", "space", None),
            P("tm", "space", None),
            P(),
            P("tm", None),
        ),
        out_specs=P("tm", "space", None),
        check_vma=False,
    )
```

```python
import functools

import jax
import jax.numpy as jnp
from jax import lax
from jax.experimental import pallas as pl
from jax.experimental.pallas import tpu as pltpu
from jax.sharding import PartitionSpec as P

HEADS = 20
LANES = 128
EARLY = (9, 14)
BEFORE_SUM = 1
PER_HOP = 1
MESH = pl.DeviceIdType.MESH


def exchange_kernel(
    n, space, k_ref, v_ref, q_ref, w_ref, gain_ref, normed_ref, wg_ref,
    keys, vals, asks, mixed, ones, state_ref, part_ref, landed, totals, arrived,
    local_sem, load_sem, rs_send, rs_recv, scan_send, scan_recv, ag_send, ag_recv,
    tm_send, tm_recv, y_send, y_recv, core_send, core_recv,
):
    t = lax.axis_index("tm")
    s = lax.axis_index("space")
    cores = 2
    ys = space // cores
    y, c = s // cores, s % cores
    bits = []
    d = 1
    while d < n:
        bits.append(d)
        d *= 2

    def flip(m):
        where = t
        for d in bits:
            if m & d:
                where = where + d - 2 * d * ((t // d) % 2)
        return where

    def peer(r):
        return (t, lax.rem(s + r, space))

    loads = [
        pltpu.make_async_copy(k_ref, keys, load_sem.at[0]),
        pltpu.make_async_copy(v_ref, vals, load_sem.at[1]),
        pltpu.make_async_copy(q_ref, asks, load_sem.at[2]),
    ]
    for load in loads:
        load.start()

    barrier = pltpu.get_barrier_semaphore()
    for r in range(1, space):
        pl.semaphore_signal(barrier, inc=1, device_id=peer(r), device_id_type=MESH)
    for d in bits:
        pl.semaphore_signal(barrier, inc=1, device_id=(flip(d), s), device_id_type=MESH)
    pl.semaphore_wait(barrier, space - 1 + len(bits))

    sent = []

    def remote(src, dst, send, recv, device):
        return pltpu.make_async_remote_copy(
            src_ref=src, dst_ref=dst, send_sem=send, recv_sem=recv,
            device_id=device, device_id_type=MESH,
        )

    def go(copy):
        copy.start()
        sent.append(copy)

    groups = (s, space + c)

    def weight_hop(i, m, d):
        g = groups[i]
        src = w_ref.at[g] if m == 0 else wg_ref.at[g, flip(m)]
        return remote(src, wg_ref.at[g, flip(m)], tm_send.at[i, m + d],
                      tm_recv.at[i, m + d], (flip(d), s))

    def await_weight(i, m):
        low = m & -m
        shard = wg_ref.at[groups[i], flip(m)]
        remote(shard, shard, tm_send.at[i, m], tm_recv.at[i, m], (flip(low), s)).wait_recv()

    def to_core(i, g, m):
        shard = wg_ref.at[g, flip(m)]
        return remote(shard, shard, core_send.at[i, m], core_recv.at[i, m],
                      (t, y * cores + (1 - c)))

    def to_y(r, m):
        shard = wg_ref.at[s, flip(m)]
        return remote(shard, shard, y_send.at[r, m], y_recv.at[r, m],
                      (t, lax.rem(y + r, ys) * cores + c))

    def from_y(r):
        return lax.rem(y + ys - r, ys) * cores + c

    for d in reversed(bits):
        for i in range(2):
            go(weight_hop(i, 0, d))
    own = pltpu.make_async_copy(w_ref, wg_ref.at[:, t], local_sem)
    own.start()

    pending = []

    def pass_on(m):
        for i in range(2):
            await_weight(i, m)
            for d in reversed(bits):
                if d < (m & -m):
                    go(weight_hop(i, m, d))
            if i == 0:
                for r in range(1, ys):
                    go(to_y(r, m))
            go(to_core(i, groups[i], m))
        pending.append(m)

    def settle(m):
        for r in range(1, ys):
            shard = wg_ref.at[from_y(r), flip(m)]
            remote(shard, shard, y_send.at[r, m], y_recv.at[r, m],
                   (t, lax.rem(y + ys - r, ys) * cores + c)).wait_recv()
            go(to_core(1 + r, from_y(r), m))

    order = sorted(range(1, n), key=lambda m: (bin(m).count("1"), -m))
    order = list(order)

    def next_weight():
        if order:
            pass_on(order.pop(0))

    heads, dim, _ = keys.shape
    ones[...] = jnp.ones_like(ones)
    for load in loads[:2]:
        load.wait()
    share = part_ref.shape[1]

    def one_state(h):
        v = jnp.concatenate([vals[h], ones[...]], axis=0)
        fk = jnp.maximum(keys[h], 0)
        return lax.dot_general(
            v, fk, (((1,), (1,)), ((), ())), preferred_element_type=jnp.float32
        ).astype(part_ref.dtype)

    for h in range(space * share):
        part_ref[h // share, h % share] = (
            one_state(h) if h < heads else jnp.zeros(part_ref.shape[2:], part_ref.dtype)
        )
        if h in EARLY:
            next_weight()

    for r in range(1, space):
        go(remote(part_ref.at[lax.rem(s + r, space)], landed.at[r],
                  rs_send.at[r], rs_recv.at[r], peer(r)))

    for _ in range(BEFORE_SUM):
        next_weight()
    total = part_ref[s].astype(jnp.float32)
    for r in range(1, space):
        remote(part_ref.at[0], landed.at[r], rs_send.at[r], rs_recv.at[r], peer(r)).wait_recv()
        total = total + landed[r].astype(jnp.float32)
    prefix = total
    for k, d in enumerate(bits):
        totals[k] = total.astype(totals.dtype)
        hop = remote(totals.at[k], arrived.at[k], scan_send.at[k], scan_recv.at[k], (flip(d), s))
        go(hop)
        for _ in range(PER_HOP):
            next_weight()
        hop.wait_recv()
        got = arrived[k].astype(jnp.float32)
        prefix = prefix + got * ((t // d) % 2).astype(jnp.float32)
        total = total + got
    state_ref[s] = prefix.astype(state_ref.dtype)
    for r in range(1, space):
        go(remote(state_ref.at[s], state_ref.at[s], ag_send.at[r], ag_recv.at[r], peer(r)))
    while order:
        next_weight()
        if len(pending) > 1:
            settle(pending.pop(0))
    for r in range(1, space):
        slot = state_ref.at[lax.rem(s + space - r, space)]
        remote(slot, slot, ag_send.at[r], ag_recv.at[r], peer(r)).wait_recv()
    loads[2].wait()
    rows = asks.shape[2]
    squares = jnp.zeros((1, rows), jnp.float32)
    for h in range(heads):
        both = jnp.dot(
            state_ref[h // share, h % share],
            jnp.maximum(asks[h], 0),
            preferred_element_type=jnp.float32,
        )
        tile = both[:dim] / (both[dim : dim + 1] + 1.0)
        mixed[h] = tile
        squares = squares + jnp.sum(tile * tile, axis=0, keepdims=True)
    while pending:
        settle(pending.pop(0))
    scale = lax.rsqrt(squares / (heads * dim) + 1e-06)
    gain = jnp.broadcast_to(gain_ref[...], (8, heads * dim)).T
    for h in range(heads):
        mixed[h] = mixed[h] * scale * gain[h * dim : (h + 1) * dim, :1]
    normed_ref[...] = mixed[...].reshape(heads * dim, rows).astype(normed_ref.dtype).T
    other = 1 - c
    for m in range(1, n):
        sources = [y * cores + other, space + other]
        sources += [lax.rem(y + ys - r, ys) * cores + other for r in range(1, ys)]
        for i, g in enumerate(sources):
            shard = wg_ref.at[g, flip(m)]
            remote(shard, shard, core_send.at[i, m], core_recv.at[i, m],
                   (t, y * cores + other)).wait_recv()
    own.wait()
    for copy in sent:
        copy.wait_send()


def project_kernel(normed_ref, w_ref, out_ref):
    out_ref[...] = (
        jnp.dot(
            normed_ref[...],
            jnp.concatenate([w_ref[0], w_ref[1]], axis=1),
            preferred_element_type=jnp.float32,
        )
        .astype(out_ref.dtype)
        .T
    )


def local(n, space, queries, keys, values, gain, out_weight):
    _, rows, width = queries.shape
    dim = width // HEADS
    extra = 16
    share = -(-HEADS // space)
    shard, columns = out_weight.shape
    groups = space + 2
    gw = -(-columns // (groups * LANES)) * LANES
    vmem = pl.BlockSpec(memory_space=pltpu.VMEM)
    big = pltpu.CompilerParams(vmem_limit_bytes=56 * 1024 * 1024)

    w = jnp.pad(out_weight, ((0, 0), (0, groups * gw - columns)))
    w = w.reshape(shard, groups, gw).transpose(1, 0, 2)

    def by_head(a):
        return a[0].T.reshape(HEADS, dim, rows)

    steps = n.bit_length() - 1
    dma = pltpu.SemaphoreType.DMA
    piece = (share, dim + extra, dim)
    normed, wg = pl.pallas_call(
        functools.partial(exchange_kernel, n, space),
        out_shape=(
            jax.ShapeDtypeStruct((rows, width), jnp.bfloat16),
            jax.ShapeDtypeStruct((groups, n, shard, gw), jnp.bfloat16),
        ),
        in_specs=[pl.BlockSpec(memory_space=pl.ANY)] * 4 + [vmem],
        out_specs=(vmem, pl.BlockSpec(memory_space=pl.ANY)),
        scratch_shapes=[
            pltpu.VMEM((HEADS, dim, rows), jnp.bfloat16),
            pltpu.VMEM((HEADS, dim, rows), jnp.bfloat16),
            pltpu.VMEM((HEADS, dim, rows), jnp.bfloat16),
            pltpu.VMEM((HEADS, dim, rows), jnp.float32),
            pltpu.VMEM((extra, rows), jnp.bfloat16),
            pltpu.VMEM((space,) + piece, jnp.bfloat16),
            pltpu.VMEM((space,) + piece, jnp.bfloat16),
            pltpu.VMEM((space,) + piece, jnp.bfloat16),
            pltpu.VMEM((steps,) + piece, jnp.bfloat16),
            pltpu.VMEM((steps,) + piece, jnp.bfloat16),
            dma,
            dma((3,)),
            dma((space,)), dma((space,)),
            dma((steps,)), dma((steps,)),
            dma((space,)), dma((space,)),
            dma((2, n)), dma((2, n)),
            dma((space // 2, n)), dma((space // 2, n)),
            dma((space // 2 + 1, n)), dma((space // 2 + 1, n)),
        ],
        compiler_params=pltpu.CompilerParams(
            collective_id=0, has_side_effects=True, vmem_limit_bytes=56 * 1024 * 1024
        ),
        name="exchange",
    )(by_head(keys), by_head(values), by_head(queries), w, gain.reshape(1, width))

    out = pl.pallas_call(
        project_kernel,
        grid=(-(-columns // (2 * gw)),),
        out_shape=jax.ShapeDtypeStruct((columns, rows), jnp.bfloat16),
        in_specs=[
            pl.BlockSpec((rows, width), lambda i: (0, 0)),
            pl.BlockSpec((2, n * shard, gw), lambda i: (i, 0, 0)),
        ],
        out_specs=pl.BlockSpec((2 * gw, rows), lambda i: (i, 0)),
        compiler_params=big,
        name="project",
    )(normed, wg.reshape(groups, n * shard, gw))
    return out.T[None]


def solution(mesh):
    sizes = dict(mesh.shape)
    return jax.shard_map(
        functools.partial(local, sizes["tm"], sizes["space"]),
        mesh=mesh,
        in_specs=(
            P("tm", "space", None),
            P("tm", "space", None),
            P("tm", "space", None),
            P(),
            P("tm", None),
        ),
        out_specs=P("tm", "space", None),
        check_vma=False,
    )
```
